256 devices in a mesh: group: 8 (over y_lo, x), blk: 32 (over y_hi, z, core).
Axes of the slice: x: 4, y: 4 (y_hi: 2, y_lo: 2; y = y_hi * 2 + y_lo), z: 8, core: 2. Of those that a mesh axis runs over, the one named last changes fastest.
Arguments:
- embeddings: bfloat16 [49152, 1024], P(('group', 'blk')), may hold values from -8 to 8
- block_cluster: int32 [3072], P(('group', 'blk')), may hold values from 0 to 24575, as said below
Outputs:
- best_match: float32 [49152], P(('group', 'blk'))
The draws below stay inside these ranges and needn't reach their ends.
Inputs may be any that keep to these rules, and one draw needn't show every extreme that they name: `block_cluster`: among the 12 blocks of one device at most 3 have cluster ids of one remainder modulo 8. Every cluster has at most 128 blocks.
All inputs are finite; a program needn't handle non-finite values.
Results may differ from the reference program's by a relative error of at most 0.00055.
Values may be sent and summed in bfloat16 or wider, within the bound.
A program may use at most 64 MiB of HBM per device.

```python
import math
import jax
import jax.numpy as jnp
from jax import lax

D = 1024
RB = 16
NB = 12
CAP = 3
GROUPS = 8
BLKS = 32
ROWS = 49152
BLOCKS = 3072
CB = 128
DEVICES = 256


def cluster_layout(key):
    key_favor, key_rest, key_order, key_rank = jax.random.split(key, 4)
    favored = jax.random.randint(key_favor, (BLKS,), 0, GROUPS)
    favored = favored.at[0].set(GROUPS - 1)
    favored_device = favored[jnp.arange(DEVICES) % BLKS]
    rest_keys = jax.random.split(key_rest, DEVICES)
    order_keys = jax.random.split(key_order, DEVICES)

    def device_groups(rest_key, order_key, favor):
        others = jax.random.permutation(rest_key, (GROUPS - 1) * CAP)[:NB - CAP] + CAP
        chosen = jnp.concatenate([jnp.arange(CAP), others])
        groups = (chosen // CAP + favor) % GROUPS
        return groups[jax.random.permutation(order_key, NB)]
    helper = jax.vmap(device_groups)(rest_keys, order_keys, favored_device).reshape(BLOCKS).astype(jnp.int32)
    shuffle = jax.random.permutation(key_rank, BLOCKS)
    matches = (helper[shuffle][:, None] == jnp.arange(GROUPS)[None, :]).astype(jnp.int32)
    counted = jnp.sum(jnp.cumsum(matches, axis=0) * matches, axis=1) - 1
    ordinal = jnp.zeros((BLOCKS,), jnp.int32).at[shuffle].set(counted.astype(jnp.int32))
    return (helper + GROUPS * (BLOCKS - 1 - ordinal // CB)).astype(jnp.int32)


def draw_block_cluster(key, part):
    return cluster_layout(key)


def draw_embeddings(key, part):
    row_ids = jnp.repeat(cluster_layout(key), RB)
    key = jax.random.fold_in(key, 7)
    key_center, key_scale, key_noise = jax.random.split(key, 3)
    centers = jax.vmap(lambda ident: jax.random.normal(jax.random.fold_in(key_center, ident), (D,), jnp.float32))(row_ids)
    scales = jnp.exp(jax.random.uniform(key_scale, (ROWS, 1), jnp.float32, minval=math.log(0.1), maxval=0.0))
    noise = jax.random.normal(key_noise, (ROWS, D), jnp.float32)
    return jnp.clip(scales * centers + noise, -8.0, 8.0).astype(jnp.bfloat16)


def setup_inputs(seed: int = 0) -> dict:
    splits = jax.random.split(jax.random.key(seed), 3)
    return {
        "embeddings": draw_embeddings(jax.random.fold_in(splits[2], 71), 0),
        "block_cluster": draw_block_cluster(jax.random.fold_in(splits[2], 71), 0),
    }


def reference(embeddings, block_cluster):
    as_float = embeddings.astype(jnp.float32)
    normed = (as_float * lax.rsqrt(lax.optimization_barrier(jnp.sum(as_float * as_float, axis=1, keepdims=True)) + 1e-06)).astype(jnp.bfloat16)
    row_cluster = jnp.repeat(block_cluster, RB).astype(jnp.int32)
    ranking = jnp.argsort(row_cluster, stable=True).astype(jnp.int32)
    sorted_rows = normed[ranking]
    sorted_ids = row_cluster[ranking]
    margin = CB * RB
    tile_rows = 512
    padded_rows = jnp.pad(sorted_rows, ((margin, margin), (0, 0)))
    padded_ids = jnp.pad(sorted_ids, (margin, margin), constant_values=-2)

    def one_tile(tile_number):
        first_row = (tile_number * tile_rows).astype(jnp.int32)
        rows_here = lax.dynamic_slice_in_dim(sorted_rows, first_row, tile_rows, 0)
        ids_here = lax.dynamic_slice_in_dim(sorted_ids, first_row, tile_rows, 0)
        window = lax.dynamic_slice_in_dim(padded_rows, first_row, tile_rows + 2 * margin, 0)
        window_ids = lax.dynamic_slice_in_dim(padded_ids, first_row, tile_rows + 2 * margin, 0)
        scores = jnp.dot(rows_here, window.T, preferred_element_type=jnp.float32)
        mine = first_row + jnp.arange(tile_rows, dtype=jnp.int32)
        theirs = first_row - margin + jnp.arange(tile_rows + 2 * margin, dtype=jnp.int32)
        allowed = (ids_here[:, None] == window_ids[None, :]) & (mine[:, None] != theirs[None, :])
        return lax.optimization_barrier(jnp.max(jnp.where(allowed, scores, -jnp.inf), axis=1))
    best_sorted = lax.map(one_tile, jnp.arange(ROWS // tile_rows, dtype=jnp.int32)).reshape(ROWS)
    return jnp.zeros((ROWS,), jnp.float32).at[ranking].set(best_sorted)
```

```python
import jax
import jax.numpy as jnp
from jax import lax
from jax.experimental import pallas as pl
from jax.experimental.pallas import tpu as pltpu
from jax.sharding import PartitionSpec as P

MESH = pl.DeviceIdType.MESH
SIZES = (4, 4, 8)
ROWS = 192
CHIP = 2 * ROWS
BLOCK = 16
BLOCKS = ROWS // BLOCK
WIDTH = 1024
LANES = 128
NEG = float("-inf")
NT = (((1,), (1,)), ((), ()))

OFFSETS = (
    (0, 0, 0),
    (0, 1, 7),
    (0, 0, 7),
    (0, 1, 0),
    (1, 3, 0),
    (2, 3, 0),
    (3, 3, 0),
    (0, 0, 1),
    (0, 0, 2),
    (1, 0, 2),
    (2, 0, 2),
    (3, 0, 2),
    (0, 1, 5),
    (0, 1, 6),
    (0, 2, 6),
    (0, 0, 6),
)
PARENTS = (
    (-1, 3, 1, 0, 5, 6, 0, 0, 7, 8, 9, 8, 13, 1, 13, 13),
    (-1, 13, 0, 0, 5, 6, 0, 0, 7, 8, 11, 8, 13, 15, 13, 2),
    (-1, 3, 1, 0, 0, 4, 5, 0, 7, 8, 11, 8, 13, 1, 13, 13),
    (-1, 2, 0, 0, 0, 4, 5, 0, 7, 8, 9, 8, 13, 15, 13, 2),
)
FIRST = (
    (0, 6), (0, 3), (0, 7), (1, 2), (2, 4), (1, 6), (2, 3), (1, 7),
    (3, 2), (3, 4), (1, 3), (2, 7), (3, 7), (3, 3),
)
PROGRAM = (
    (2, 1), (3, 0), (7, 0), (4, 2), (6, 0), (2, 3), (3, 2), (7, 1), (4, 3), (6, 1),
    (1, 0), (3, 1), (7, 2), (5, 0), (5, 2), (1, 3), (7, 3), (15, 1), (5, 1), (5, 3),
    (2, 0), (1, 2), (3, 3), (8, 0), (4, 0), (6, 2), (8, 1), (13, 1), (15, 3), (4, 1),
    (6, 3), (-1, 0), (2, 2), (8, 2), (13, 0), (9, 0), (11, 0), (-1, 1), (-1, 2), (14, 1),
    (8, 3), (13, 2), (9, 1), (11, 1), (-1, 3), (13, 3), (15, 0), (1, 1), (12, 0), (10, 0),
    (11, 2), (-1, 4), (14, 0), (15, 2), (12, 1), (9, 3), (10, 1), (-1, 5), (-1, 6), (14, 2),
    (12, 2), (9, 2), (10, 2), (-1, 7), (-1, 8), (14, 3), (12, 3), (10, 3), (11, 3), (-1, 9),
    (-1, 10), (-1, 11), (-1, 12), (-1, 13), (-1, 14), (-1, 15), (-1, 16),
)
STEPS = (
    ((0, 7, 0, 5), (5, 7, 0, 3),),
    ((3, 7, 3, 5), (0, 4, 0, 6),),
    ((4, 7, 6, 7), (4, 5, 3, 4),),
    ((4, 6, 2, 7), (2, 5, 2, 3),),
    ((2, 4, 2, 6), (5, 8, 3, 8),),
    ((4, 8, 6, 8), (2, 8, 7, 13),),
    ((5, 13, 4, 13), (6, 13, 8, 13),),
    ((1, 5, 1, 4), (1, 6, 5, 15),),
    ((3, 15, 4, 15), (6, 15, 8, 15),),
    ((0, 9, 7, 9), (2, 9, 9, 13),),
    ((1, 9, 9, 15), (0, 14, 7, 14),),
    ((2, 14, 8, 14), (14, 15, 9, 14),),
    ((5, 12, 4, 12), (6, 12, 8, 12),),
    ((9, 12, 0, 10), (0, 11, 7, 10),),
    ((7, 11, 2, 10), (2, 11, 10, 13),),
    ((11, 13, 1, 10), (1, 11, 10, 15),),
    ((10, 14, 10, 12), (11, 12, 10, 12),),
)

SLOTS = len(OFFSETS)
PARTS = len(PARENTS)
PART = ROWS // PARTS


def minus(a, b):
    return tuple((p - q) % m for p, q, m in zip(a, b, SIZES))


ORIGIN = (0, 0, 0)


def partners():
    found = {(ORIGIN, 1)}
    for offset in OFFSETS[1:]:
        for flip in (0, 1):
            found.add((offset, flip))
            found.add((minus(ORIGIN, offset), flip))
    for parents in PARENTS:
        for slot in range(1, SLOTS):
            hop = minus(OFFSETS[parents[slot]], OFFSETS[slot])
            found.add((hop, 0))
            found.add((minus(ORIGIN, hop), 0))
    return sorted(found)


def kernel(
    ids_ref, emb_ref, out_ref,
    buf, idb, idcol, idrow, racc, cacc, mat, res, rin,
    data_s, data_r, swap_s, swap_r, id_s, id_r, ret_s, ret_r,
):
    group = lax.axis_index("group")
    blk = lax.axis_index("blk")
    core = lax.rem(blk, 2)
    place = (lax.rem(group, 4), (blk // 16) * 2 + group // 4, lax.rem(blk // 2, 8))

    def device(offset, flip):
        x, y, z = (lax.rem(p + o, m) if o else p for p, o, m in zip(place, offset, SIZES))
        there = 1 - core if flip else core
        return (lax.rem(y, 2) * 4 + x, (y // 2) * 16 + z * 2 + there)

    barrier = pltpu.get_barrier_semaphore()
    everyone = partners()
    for offset, flip in everyone:
        pl.semaphore_signal(barrier, inc=1, device_id=device(offset, flip), device_id_type=MESH)

    def rows_of(slot, part, count):
        return pl.ds(pl.multiple_of(slot * CHIP + core * ROWS + part * PART, BLOCK), count)

    own = rows_of(0, 0, ROWS)
    as_float = emb_ref[...].astype(jnp.float32)
    total = jnp.sum(as_float * as_float, axis=1, keepdims=True)
    buf[own, :] = (as_float * lax.rsqrt(total + 1e-06)).astype(jnp.bfloat16)
    for block in range(BLOCKS):
        idb[0, core, pl.ds(block, 1), :] = jnp.full((1, LANES), ids_ref[block], jnp.int32)
    idb[0, core, pl.ds(BLOCKS, BLOCK - BLOCKS), :] = jnp.full((BLOCK - BLOCKS, LANES), -1, jnp.int32)
    pl.semaphore_wait(barrier, len(everyone))

    def id_copy(slot, flip):
        return pltpu.make_async_remote_copy(
            src_ref=idb.at[0, core], dst_ref=idb.at[slot, core], send_sem=id_s.at[slot, flip], recv_sem=id_r.at[slot, core],
            device_id=device(minus(ORIGIN, OFFSETS[slot]), flip), device_id_type=MESH)

    def data_copy(slot, part):
        parent = PARENTS[part][slot]
        return pltpu.make_async_remote_copy(
            src_ref=buf.at[rows_of(parent, part, PART), :], dst_ref=buf.at[rows_of(slot, part, PART), :],
            send_sem=data_s.at[slot, part], recv_sem=data_r.at[slot, part],
            device_id=device(minus(OFFSETS[parent], OFFSETS[slot]), 0), device_id_type=MESH)

    def swap_copy(slot):
        return pltpu.make_async_remote_copy(
            src_ref=buf.at[rows_of(slot, 0, ROWS), :], dst_ref=buf.at[rows_of(slot, 0, ROWS), :],
            send_sem=swap_s.at[slot], recv_sem=swap_r.at[slot], device_id=device(ORIGIN, 1), device_id_type=MESH)

    def return_copy(slot, flip):
        return pltpu.make_async_remote_copy(
            src_ref=res.at[pl.ds(slot, 1), :], dst_ref=rin.at[pl.ds(slot * 2 + core, 1), :],
            send_sem=ret_s.at[slot, flip], recv_sem=ret_r.at[slot, core],
            device_id=device(OFFSETS[slot], flip), device_id_type=MESH)

    fan = [(slot, flip) for slot in range(SLOTS) for flip in (0, 1) if (slot, flip) != (0, 0)]
    for slot, flip in fan:
        id_copy(slot, flip).start()
    for part, slot in FIRST:
        data_copy(slot, part).start()
    swap_copy(0).start()

    racc[...] = jnp.full(racc.shape, NEG, jnp.float32)
    cacc[...] = jnp.full(cacc.shape, NEG, jnp.float32)

    def wait_id(slot, sender):
        pltpu.make_async_remote_copy(
            src_ref=idb.at[0, core], dst_ref=idb.at[slot, sender], send_sem=id_s.at[slot, 0], recv_sem=id_r.at[slot, sender],
            device_id=device(ORIGIN, 1), device_id_type=MESH).wait_recv()

    wait_id(0, 1 - core)
    for slot in range(1, SLOTS):
        for sender in (0, 1):
            wait_id(slot, sender)

    lane = lax.broadcasted_iota(jnp.int32, (1, CHIP), 1)

    def prepare(slot, carry):
        row = jnp.zeros((1, CHIP), jnp.int32)
        for half in (0, 1):
            tile = idb[slot, half]
            for block in range(BLOCKS):
                splat = tile[block:block + 1, :]
                at = half * ROWS + block * BLOCK
                idcol[pl.ds(pl.multiple_of(slot * CHIP, CHIP) + at, BLOCK), :] = jnp.broadcast_to(splat, (BLOCK, LANES))
                row = jnp.where(lane // BLOCK == at // BLOCK, jnp.concatenate([splat] * 3, axis=1), row)
        idrow[pl.ds(pl.multiple_of(slot * 8, 8), 8), :] = jnp.broadcast_to(row, (8, CHIP))
        return carry

    lax.fori_loop(0, SLOTS, prepare, 0)

    def merge(first, second, count, itself):
        left = pl.ds(pl.multiple_of(first, BLOCK), count)
        right = pl.ds(pl.multiple_of(second * CHIP, CHIP), CHIP)
        top = pl.ds(pl.multiple_of(second * 8, 8), 8)
        scores = lax.dot_general(buf[left, :], buf[right, :], NT, preferred_element_type=jnp.float32)
        mine = idcol[left, :]
        theirs = idrow[pl.ds(pl.multiple_of(second * 8, 8), 1), :]
        best = racc[left, :]
        tops = []
        for tile in range(CHIP // LANES):
            cut = slice(tile * LANES, (tile + 1) * LANES)
            allowed = mine == theirs[:, cut]
            if itself:
                here = lax.broadcasted_iota(jnp.int32, (count, LANES), 0) + first
                there = lax.broadcasted_iota(jnp.int32, (count, LANES), 1) + tile * LANES
                allowed = allowed & (here != there)
            kept = jnp.where(allowed, scores[:, cut], NEG)
            best = jnp.maximum(best, kept)
            if not itself:
                tops.append(jnp.max(kept.reshape(count // 8, 8, LANES), axis=0))
        racc[left, :] = best
        if not itself:
            cacc[top, :] = jnp.maximum(cacc[top, :], jnp.concatenate(tops, axis=1))

    have = set()

    def need(slot):
        if slot not in have:
            have.add(slot)
            swap_copy(slot).wait_recv()

    need(0)
    merge(core * ROWS, 0, ROWS, True)

    arrived = [0] * SLOTS
    for slot, index in PROGRAM:
        if slot >= 0:
            data_copy(slot, index).wait_recv()
            for child in range(1, SLOTS):
                if PARENTS[index][child] == slot:
                    data_copy(child, index).start()
            arrived[slot] += 1
            if arrived[slot] == PARTS:
                swap_copy(slot).start()
        else:
            for one in STEPS[index]:
                for other in one:
                    need(other)
            for p0, q0, p1, q1 in STEPS[index]:
                merge((p0 + core * (p1 - p0)) * CHIP, q0 + core * (q1 - q0), CHIP, False)

    lanes = lax.broadcasted_iota(jnp.int32, (CHIP, LANES), 1)
    mat[...] = jnp.full(mat.shape, NEG, jnp.float32)

    def reduce(slot, carry):
        wide = racc[pl.ds(pl.multiple_of(slot * CHIP, CHIP), CHIP), :]
        mat[...] = jnp.where(lanes == slot, jnp.max(wide, axis=1, keepdims=True), mat[...])
        return carry

    lax.fori_loop(0, SLOTS, reduce, 0)
    turned = jnp.transpose(mat[...])[:SLOTS]
    res[...] = jnp.maximum(turned, jnp.max(cacc[...].reshape(SLOTS, 8, CHIP), axis=1))

    for slot, flip in reversed(fan):
        return_copy(slot, flip).start()
    rin[pl.ds(core, 1), :] = res[pl.ds(0, 1), :]

    def wait_return(slot, sender):
        pltpu.make_async_remote_copy(
            src_ref=res.at[pl.ds(slot, 1), :], dst_ref=rin.at[pl.ds(slot * 2 + sender, 1), :],
            send_sem=ret_s.at[slot, 0], recv_sem=ret_r.at[slot, sender],
            device_id=device(ORIGIN, 1), device_id_type=MESH).wait_recv()

    wait_return(0, 1 - core)
    for slot in range(1, SLOTS):
        for sender in (0, 1):
            wait_return(slot, sender)
    joined = jnp.max(rin[...], axis=0, keepdims=True)
    out_ref[...] = jnp.where(core == 0, joined[:, :ROWS], joined[:, ROWS:])

    for slot, flip in fan:
        id_copy(slot, flip).wait_send()
        return_copy(slot, flip).wait_send()
    swap_copy(0).wait_send()
    for slot in range(1, SLOTS):
        for part in range(PARTS):
            data_copy(slot, part).wait_send()
        swap_copy(slot).wait_send()


def per_device(embeddings, block_cluster):
    vmem = pl.BlockSpec(memory_space=pltpu.VMEM)
    dma = pltpu.SemaphoreType.DMA
    out = pl.pallas_call(
        kernel,
        out_shape=jax.ShapeDtypeStruct((1, ROWS), jnp.float32),
        in_specs=[pl.BlockSpec(memory_space=pltpu.SMEM), vmem],
        out_specs=vmem,
        scratch_shapes=[
            pltpu.VMEM((SLOTS * CHIP, WIDTH), jnp.bfloat16),
            pltpu.VMEM((SLOTS, 2, BLOCK, LANES), jnp.int32),
            pltpu.VMEM((SLOTS * CHIP, LANES), jnp.int32),
            pltpu.VMEM((SLOTS * 8, CHIP), jnp.int32),
            pltpu.VMEM((SLOTS * CHIP, LANES), jnp.float32),
            pltpu.VMEM((SLOTS * 8, CHIP), jnp.float32),
            pltpu.VMEM((CHIP, LANES), jnp.float32),
            pltpu.VMEM((SLOTS, CHIP), jnp.float32),
            pltpu.VMEM((SLOTS * 2, CHIP), jnp.float32),
            dma((SLOTS, PARTS)), dma((SLOTS, PARTS)),
            dma((SLOTS,)), dma((SLOTS,)),
            dma((SLOTS, 2)), dma((SLOTS, 2)),
            dma((SLOTS, 2)), dma((SLOTS, 2)),
        ],
        compiler_params=pltpu.CompilerParams(
            collective_id=0, has_side_effects=True, vmem_limit_bytes=40 * 2**20),
    )(block_cluster, embeddings)
    return out.reshape(ROWS)


def solution(mesh):
    return jax.shard_map(
        per_device, mesh=mesh, in_specs=(P(("group", "blk"), None), P(("group", "blk"))), out_specs=P(("group", "blk")),
        check_vma=False,
    )
```

```python
import jax
import jax.numpy as jnp
from jax import lax
from jax.experimental import pallas as pl
from jax.experimental.pallas import tpu as pltpu
from jax.sharding import PartitionSpec as P

MESH = pl.DeviceIdType.MESH
SIZES = (4, 4, 8)
ROWS = 192
CHIP = 2 * ROWS
BLOCK = 16
BLOCKS = ROWS // BLOCK
WIDTH = 1024
LANES = 128
NEG = float("-inf")
NT = (((1,), (1,)), ((), ()))

SEND, SWAP, STEP, FOLD = range(4)
OFFSETS = (
    (0, 0, 0), (0, 0, 7), (1, 0, 7), (2, 0, 7), (3, 0, 7), (2, 0, 0), (0, 1, 0), (3, 1, 0),
    (0, 2, 0), (0, 3, 0), (0, 0, 2), (0, 1, 2), (0, 2, 2), (0, 3, 2), (0, 0, 6), (1, 0, 6),
    (2, 0, 6),
)
PARENTS = (
    (-1, 0, 1, 2, 3, 3, 0, 6, 6, 0, 0, 12, 13, 10, 15, 16, 3),
    (-1, 0, 3, 5, 1, 0, 0, 6, 6, 0, 13, 10, 13, 9, 4, 2, 15),
    (-1, 0, 1, 5, 3, 0, 0, 6, 6, 0, 13, 10, 13, 9, 15, 2, 15),
    (-1, 0, 1, 2, 1, 3, 0, 6, 9, 0, 0, 10, 13, 10, 1, 2, 3),
)
PROGRAM = (
    (SEND, 1, 0), (SEND, 5, 1), (SEND, 6, 0), (SEND, 9, 0), (SEND, 10, 0), (SWAP, 0, 0), (SEND, 5, 2),
    (SEND, 1, 3), (SEND, 6, 3), (SEND, 9, 2), (SEND, 1, 2), (SEND, 6, 2), (SEND, 9, 3), (SEND, 10, 3),
    (SEND, 2, 0), (SEND, 7, 0), (SEND, 6, 1), (SEND, 9, 1), (SEND, 3, 1), (SEND, 2, 3), (SEND, 7, 3),
    (SEND, 8, 0), (SEND, 3, 2), (SEND, 13, 2), (SEND, 13, 0), (SEND, 2, 2), (SEND, 7, 2), (SEND, 1, 1),
    (SEND, 8, 2), (SEND, 8, 3), (SEND, 3, 0), (SWAP, 6, 0), (SWAP, 9, 0), (SEND, 7, 1), (SEND, 8, 1),
    (SEND, 13, 1), (SEND, 15, 3), (SEND, 13, 3), (SEND, 2, 1), (SEND, 3, 3), (SEND, 11, 3), (SEND, 12, 0),
    (SEND, 15, 2), (SEND, 4, 3), (SEND, 4, 2), (SWAP, 1, 0), (SWAP, 7, 0), (SEND, 10, 2), (SEND, 12, 2),
    (SEND, 16, 0), (SEND, 5, 0), (SEND, 4, 1), (SEND, 4, 0), (SWAP, 8, 0), (STEP, 0, 0), (SEND, 12, 3),
    (SWAP, 2, 0), (SEND, 15, 1), (SWAP, 3, 0), (SEND, 5, 3), (STEP, 1, 0), (SEND, 14, 2), (SEND, 16, 2),
    (SEND, 14, 3), (SEND, 11, 0), (SEND, 10, 1), (SWAP, 13, 0), (STEP, 2, 0), (STEP, 3, 0), (SEND, 15, 0),
    (SEND, 11, 2), (SEND, 14, 1), (SEND, 12, 1), (SWAP, 4, 0), (STEP, 4, 0), (SEND, 16, 1), (SWAP, 5, 0),
    (SEND, 16, 3), (STEP, 5, 0), (SEND, 11, 1), (SWAP, 10, 0), (STEP, 6, 0), (STEP, 7, 0), (SEND, 14, 0),
    (SWAP, 15, 0), (STEP, 8, 0), (SWAP, 12, 0), (STEP, 9, 0), (STEP, 10, 0), (STEP, 11, 0), (STEP, 12, 0),
    (STEP, 13, 0), (FOLD, 0, 0), (STEP, 14, 0), (STEP, 15, 0), (STEP, 16, 0), (STEP, 17, 0), (STEP, 18, 0),
    (STEP, 19, 0), (STEP, 20, 0),
)
STEPS = (
    ((6, 0, 6, 9), (1, 0, 1, 6),),
    ((1, 9, 7, 0), (7, 6, 7, 9),),
    ((7, 1, 8, 1), (8, 7, 2, 0),),
    ((2, 9, 2, 8), (3, 0, 3, 1),),
    ((3, 6, 3, 9), (3, 7, 3, 8),),
    ((13, 0, 13, 1), (13, 6, 13, 7),),
    ((13, 8, 13, 9), (13, 2, 13, 3),),
    ((4, 0, 4, 8), (4, 9, 4, 13),),
    ((5, 6, 5, 8), (5, 13, 10, 1),),
    ((10, 2, 10, 3), (10, 7, 10, 4),),
    ((10, 5, 15, 0), (15, 5, 15, 6),),
    ((15, 7, 15, 8), (15, 9, 15, 13),),
    ((15, 10, 12, 1), (12, 2, 12, 3),),
    ((12, 4, 12, 5),),
    ((12, 7), (12, 15),),
    ((11, 1), (11, 2),),
    ((11, 3), (11, 4),),
    ((11, 15), (16, 10),),
    ((16, 13), (16, 12),),
    ((14, 10), (14, 12),),
    ((14, 13),),
)

SLOTS = len(OFFSETS)
PARTS = len(PARENTS)
PART = ROWS // PARTS


def minus(a, b):
    return tuple((p - q) % m for p, q, m in zip(a, b, SIZES))


ORIGIN = (0, 0, 0)


def partners():
    found = {(ORIGIN, 1)}
    for parents in PARENTS:
        for slot in range(1, SLOTS):
            hop = minus(OFFSETS[parents[slot]], OFFSETS[slot])
            found.add((hop, 0))
            found.add((minus(ORIGIN, hop), 0))
    return sorted(found)


def kernel(
    ids_ref, emb_ref, out_ref,
    emb, ids, buf, idb, idcol, idrow, racc, cacc, mat, res, rin,
    load, data_s, data_r, swap_s, swap_r, id_s, id_r, ids_s, ids_r, ret_s, ret_r,
):
    loads = [pltpu.make_async_copy(emb_ref, emb, load.at[0]), pltpu.make_async_copy(ids_ref, ids, load.at[1])]
    for one in loads:
        one.start()
    group = lax.axis_index("group")
    blk = lax.axis_index("blk")
    core = lax.rem(blk, 2)
    place = (lax.rem(group, 4), (blk // 16) * 2 + group // 4, lax.rem(blk // 2, 8))

    def device(offset, flip):
        x, y, z = (lax.rem(p + o, m) if o else p for p, o, m in zip(place, offset, SIZES))
        there = 1 - core if flip else core
        return (lax.rem(y, 2) * 4 + x, (y // 2) * 16 + z * 2 + there)

    barrier = pltpu.get_barrier_semaphore()
    everyone = partners()
    for offset, flip in everyone:
        pl.semaphore_signal(barrier, inc=1, device_id=device(offset, flip), device_id_type=MESH)

    def rows_of(slot, part, count):
        return pl.ds(pl.multiple_of(slot * CHIP + core * ROWS + part * PART, BLOCK), count)

    own = rows_of(0, 0, ROWS)
    for one in loads:
        one.wait()
    as_float = emb[...].astype(jnp.float32)
    total = jnp.sum(as_float * as_float, axis=1, keepdims=True)
    buf[own, :] = (as_float * lax.rsqrt(total + 1e-06)).astype(jnp.bfloat16)
    for block in range(BLOCKS):
        idb[0, core, pl.ds(block, 1), :] = jnp.full((1, LANES), ids[block], jnp.int32)
    idb[0, core, pl.ds(BLOCKS, BLOCK - BLOCKS), :] = jnp.full((BLOCK - BLOCKS, LANES), -1, jnp.int32)
    pl.semaphore_wait(barrier, len(everyone))

    def data_copy(slot, part):
        parent = PARENTS[part][slot]
        return pltpu.make_async_remote_copy(
            src_ref=buf.at[rows_of(parent, part, PART), :], dst_ref=buf.at[rows_of(slot, part, PART), :],
            send_sem=data_s.at[slot, part], recv_sem=data_r.at[slot, part],
            device_id=device(minus(OFFSETS[parent], OFFSETS[slot]), 0), device_id_type=MESH)

    def id_copy(slot):
        parent = PARENTS[0][slot]
        return pltpu.make_async_remote_copy(
            src_ref=idb.at[parent, core], dst_ref=idb.at[slot, core], send_sem=id_s.at[slot], recv_sem=id_r.at[slot],
            device_id=device(minus(OFFSETS[parent], OFFSETS[slot]), 0), device_id_type=MESH)

    def swap_copy(slot):
        return pltpu.make_async_remote_copy(
            src_ref=buf.at[rows_of(slot, 0, ROWS), :], dst_ref=buf.at[rows_of(slot, 0, ROWS), :],
            send_sem=swap_s.at[slot], recv_sem=swap_r.at[slot], device_id=device(ORIGIN, 1), device_id_type=MESH)

    def swap_ids(slot):
        return pltpu.make_async_remote_copy(
            src_ref=idb.at[slot, core], dst_ref=idb.at[slot, core], send_sem=ids_s.at[slot], recv_sem=ids_r.at[slot],
            device_id=device(ORIGIN, 1), device_id_type=MESH)

    def return_copy(slot, flip):
        return pltpu.make_async_remote_copy(
            src_ref=res.at[pl.ds(slot, 1), :], dst_ref=rin.at[pl.ds(slot * 2 + core, 1), :],
            send_sem=ret_s.at[slot, flip], recv_sem=ret_r.at[slot, core],
            device_id=device(OFFSETS[slot], flip), device_id_type=MESH)

    fan = [(slot, flip) for slot in range(SLOTS) for flip in (0, 1) if (slot, flip) != (0, 0)]

    def merge(first, second, count, itself):
        left = pl.ds(pl.multiple_of(first, BLOCK), count)
        right = pl.ds(pl.multiple_of(second * CHIP, CHIP), CHIP)
        top = pl.ds(pl.multiple_of(second * 8, 8), 8)
        scores = lax.dot_general(buf[left, :], buf[right, :], NT, preferred_element_type=jnp.float32)
        mine = idcol[left, :]
        theirs = idrow[pl.ds(pl.multiple_of(second * 8, 8), 1), :]
        best = racc[left, :]
        tops = []
        for tile in range(CHIP // LANES):
            cut = slice(tile * LANES, (tile + 1) * LANES)
            allowed = mine == theirs[:, cut]
            if itself:
                here = lax.broadcasted_iota(jnp.int32, (count, LANES), 0) + first
                there = lax.broadcasted_iota(jnp.int32, (count, LANES), 1) + tile * LANES
                allowed = allowed & (here != there)
            kept = jnp.where(allowed, scores[:, cut], NEG)
            best = jnp.maximum(best, kept)
            if not itself:
                tops.append(jnp.max(kept.reshape(count // 8, 8, LANES), axis=0))
        racc[left, :] = best
        if not itself:
            cacc[top, :] = jnp.maximum(cacc[top, :], jnp.concatenate(tops, axis=1))

    def spread(slot, half):
        tile = idb[slot, half]
        wide = jnp.broadcast_to(tile[:BLOCKS, None, :], (BLOCKS, BLOCK, LANES)).reshape(ROWS, LANES)
        idcol[pl.ds(pl.multiple_of(slot * CHIP + half * ROWS, BLOCK), ROWS), :] = wide

    owner = lax.broadcasted_iota(jnp.int32, (8, LANES), 1) // BLOCK
    sub = lax.broadcasted_iota(jnp.int32, (8, LANES), 0)

    def across(slot):
        both = jnp.concatenate([idb[slot, 0][:BLOCKS], idb[slot, 1][:BLOCKS]], axis=0)
        tiles = [
            jnp.max(jnp.where(owner == sub, both[8 * tile:8 * tile + 8], -1), axis=0, keepdims=True)
            for tile in range(CHIP // LANES)
        ]
        idrow[pl.ds(slot * 8, 8), :] = jnp.broadcast_to(jnp.concatenate(tiles, axis=1), (8, CHIP))

    lanes = lax.broadcasted_iota(jnp.int32, (CHIP, LANES), 1)

    def fold(slots):
        for slot in slots:
            wide = racc[pl.ds(slot * CHIP, CHIP), :]
            mat[...] = jnp.where(lanes == slot, jnp.max(wide, axis=1, keepdims=True), mat[...])

    arrived, here, have = set(), set(), set()

    def arrive(slot, part):
        if slot and (slot, part) not in arrived:
            arrived.add((slot, part))
            data_copy(slot, part).wait_recv()
            if part == 0:
                id_copy(slot).wait_recv()

    def need_half(slot):
        if slot not in here:
            here.add(slot)
            for part in range(PARTS):
                arrive(slot, part)
            spread(slot, core)

    def need(slot):
        need_half(slot)
        if slot not in have:
            have.add(slot)
            swap_copy(slot).wait_recv()
            swap_ids(slot).wait_recv()
            spread(slot, 1 - core)
            across(slot)

    swapped, started = [], False
    for kind, one, part in PROGRAM:
        if kind == SEND:
            arrive(PARENTS[part][one], part)
            if part == 0:
                id_copy(one).start()
            data_copy(one, part).start()
        elif kind == SWAP:
            for index in range(PARTS):
                arrive(one, index)
            swapped.append(one)
            swap_ids(one).start()
            swap_copy(one).start()
        elif kind == FOLD:
            late = {pair[0] for step in STEPS for pair in step if len(pair) == 2}
            fold([slot for slot in range(SLOTS) if slot not in late])
        else:
            if not started:
                started = True
                racc[...] = jnp.full(racc.shape, NEG, jnp.float32)
                cacc[...] = jnp.full(cacc.shape, NEG, jnp.float32)
                mat[...] = jnp.full(mat.shape, NEG, jnp.float32)
                need(0)
                merge(core * ROWS, 0, ROWS, True)
            for pair in STEPS[one]:
                if len(pair) == 2:
                    need_half(pair[0])
                    need(pair[1])
                else:
                    for slot in pair:
                        need(slot)
            for pair in STEPS[one]:
                if len(pair) == 2:
                    merge(pair[0] * CHIP + core * ROWS, pair[1], ROWS, False)
                else:
                    p0, q0, p1, q1 = pair
                    merge((p0 + core * (p1 - p0)) * CHIP, q0 + core * (q1 - q0), CHIP, False)

    fold(sorted(late))
    turned = jnp.transpose(mat[...])[:SLOTS]
    res[...] = jnp.maximum(turned, jnp.max(cacc[...].reshape(SLOTS, 8, CHIP), axis=1))

    for slot, flip in reversed(fan):
        return_copy(slot, flip).start()
    rin[pl.ds(core, 1), :] = res[pl.ds(0, 1), :]

    def wait_return(slot, sender):
        pltpu.make_async_remote_copy(
            src_ref=res.at[pl.ds(slot, 1), :], dst_ref=rin.at[pl.ds(slot * 2 + sender, 1), :],
            send_sem=ret_s.at[slot, 0], recv_sem=ret_r.at[slot, sender],
            device_id=device(ORIGIN, 1), device_id_type=MESH).wait_recv()

    wait_return(0, 1 - core)
    for slot in range(1, SLOTS):
        for sender in (0, 1):
            wait_return(slot, sender)
    joined = jnp.max(rin[...], axis=0, keepdims=True)
    out_ref[...] = jnp.where(core == 0, joined[:, :ROWS], joined[:, ROWS:])

    for slot, flip in fan:
        return_copy(slot, flip).wait_send()
    for slot in swapped:
        swap_ids(slot).wait_send()
        swap_copy(slot).wait_send()
    for slot in range(1, SLOTS):
        id_copy(slot).wait_send()
        for part in range(PARTS):
            data_copy(slot, part).wait_send()


def per_device(embeddings, block_cluster):
    vmem = pl.BlockSpec(memory_space=pltpu.VMEM)
    dma = pltpu.SemaphoreType.DMA
    out = pl.pallas_call(
        kernel,
        out_shape=jax.ShapeDtypeStruct((1, ROWS), jnp.float32),
        in_specs=[pl.BlockSpec(memory_space=pl.ANY)] * 2,
        out_specs=vmem,
        scratch_shapes=[
            pltpu.VMEM((ROWS, WIDTH), jnp.bfloat16),
            pltpu.SMEM((BLOCKS,), jnp.int32),
            pltpu.VMEM((SLOTS * CHIP, WIDTH), jnp.bfloat16),
            pltpu.VMEM((SLOTS, 2, BLOCK, LANES), jnp.int32),
            pltpu.VMEM((SLOTS * CHIP, LANES), jnp.int32),
            pltpu.VMEM((SLOTS * 8, CHIP), jnp.int32),
            pltpu.VMEM((SLOTS * CHIP, LANES), jnp.float32),
            pltpu.VMEM((SLOTS * 8, CHIP), jnp.float32),
            pltpu.VMEM((CHIP, LANES), jnp.float32),
            pltpu.VMEM((SLOTS, CHIP), jnp.float32),
            pltpu.VMEM((SLOTS * 2, CHIP), jnp.float32),
            dma((2,)),
            dma((SLOTS, PARTS)), dma((SLOTS, PARTS)),
            dma((SLOTS,)), dma((SLOTS,)),
            dma((SLOTS,)), dma((SLOTS,)),
            dma((SLOTS,)), dma((SLOTS,)),
            dma((SLOTS, 2)), dma((SLOTS, 2)),
        ],
        compiler_params=pltpu.CompilerParams(
            collective_id=0, has_side_effects=True, vmem_limit_bytes=40 * 2**20),
    )(block_cluster, embeddings)
    return out.reshape(ROWS)


def solution(mesh):
    return jax.shard_map(
        per_device, mesh=mesh, in_specs=(P(("group", "blk"), None), P(("group", "blk"))), out_specs=P(("group", "blk")),
        check_vma=False,
    )
```

```python
import functools

import jax
import jax.numpy as jnp
from jax import lax
from jax.experimental import pallas as pl
from jax.experimental.pallas import tpu as pltpu
from jax.sharding import PartitionSpec as P

MESH = pl.DeviceIdType.MESH
SIZES = (4, 4, 8)
ROWS = 192
CHIP = 2 * ROWS
BLOCK = 16
BLOCKS = ROWS // BLOCK
WIDTH = 1024
LANES = 128
NEG = float("-inf")
NT = (((1,), (1,)), ((), ()))

SEND, SWAP, STEP, FOLD = range(4)
OFFSETS = (
    (0, 0, 0), (3, 0, 0), (1, 1, 0), (2, 1, 0), (3, 3, 0), (0, 0, 1), (0, 1, 1), (0, 2, 1),
    (0, 3, 1), (0, 0, 2), (0, 2, 2), (0, 3, 2), (0, 0, 6), (1, 0, 6), (2, 0, 6), (3, 0, 6),
)
PARENTS = (
    (-1, 0, 0, 2, 1, 0, 5, 6, 11, 5, 11, 9, 0, 14, 15, 12),
    (-1, 0, 0, 2, 1, 0, 5, 6, 11, 5, 11, 9, 15, 12, 15, 1),
    (-1, 0, 0, 2, 0, 0, 5, 8, 0, 5, 7, 8, 0, 12, 13, 12),
)
PROGRAM = (
    (SEND, 1, 0), (SEND, 2, 0), (SEND, 5, 0), (SEND, 8, 2), (SEND, 12, 0), (SWAP, 0, 0), (SEND, 4, 2),
    (SEND, 2, 2), (SEND, 1, 1), (SEND, 2, 1), (SEND, 5, 1), (SEND, 12, 2), (SEND, 4, 0), (SEND, 1, 2),
    (SEND, 3, 0), (SEND, 6, 0), (SEND, 9, 0), (SEND, 7, 2), (SEND, 15, 0), (SEND, 3, 2), (SEND, 4, 1),
    (SEND, 6, 1), (SEND, 9, 1), (SEND, 15, 1), (SWAP, 2, 0), (SEND, 3, 1), (SEND, 5, 2), (SWAP, 1, 0),
    (SEND, 11, 0), (SEND, 7, 0), (SEND, 15, 2), (SEND, 11, 2), (SEND, 13, 2), (SWAP, 4, 0), (SEND, 11, 1),
    (SEND, 14, 0), (SEND, 7, 1), (STEP, 0, 0), (SWAP, 3, 0), (SWAP, 5, 0), (SEND, 9, 2), (SEND, 6, 2),
    (SEND, 8, 0), (SEND, 10, 0), (SEND, 12, 1), (SWAP, 15, 0), (SEND, 14, 1), (SEND, 10, 2), (STEP, 1, 0),
    (SEND, 14, 2), (SWAP, 11, 0), (SEND, 8, 1), (SEND, 10, 1), (SWAP, 7, 0), (SEND, 13, 0), (STEP, 2, 0),
    (STEP, 3, 0), (STEP, 4, 0), (SWAP, 9, 0), (SWAP, 12, 0), (SEND, 13, 1), (SWAP, 6, 0), (STEP, 5, 0),
    (STEP, 6, 0), (STEP, 7, 0), (SWAP, 8, 0), (SWAP, 14, 0), (SWAP, 10, 0), (STEP, 8, 0), (STEP, 9, 0),
    (STEP, 10, 0), (SWAP, 13, 0), (STEP, 11, 0), (STEP, 12, 0), (STEP, 13, 0), (STEP, 14, 0), (STEP, 15, 0),
    (FOLD, 0, 0), (STEP, 16, 0), (FOLD, 1, 0), (STEP, 17, 0), (FOLD, 2, 0),
)
STEPS = (
    ((2, (0, 1)), (4, (1, 2))),
    ((3, (1, 4)), (5, (3, 4))),
    ((15, (1, 4)), (15, (0, 3))),
    ((15, (2, 5)), (5, (2, 0))),
    ((11, (5, 1)), (11, (2, 3))),
    ((11, (15, 7)), (7, (0, 1))),
    ((7, (4, 2)), (7, (3, 5))),
    ((15, (7, 9)), (9, (3, 2))),
    ((12, (7, 11)), (6, (3, 15))),
    ((9, (4, 12)), (12, (1, 5))),
    ((8, (3, 15)), (6, (2, 12))),
    ((14, (0, 3)), (14, (5, 6))),
    ((14, (7, 8)), (14, (9, 11))),
    ((12, (14, 10)), (10, (0, 1))),
    ((10, (15, 14)), (13, (5, 6))),
    ((13, (7, 8)), (8, (2, 12))),
    ((13, (11,)), (1, (0,))),
    ((5, (1,)),),
)
FOLDS = ((10, 14, 3, 7, 15, 2, 4, 6, 8, 9, 12), (11, 13, 0), (1, 5))

SLOTS = len(OFFSETS)
PARTS = len(PARENTS)
PART = ROWS // PARTS


def minus(a, b):
    return tuple((p - q) % m for p, q, m in zip(a, b, SIZES))


ORIGIN = (0, 0, 0)


def partners():
    found = {(ORIGIN, 1)}
    for parents in PARENTS:
        for slot in range(1, SLOTS):
            hop = minus(OFFSETS[parents[slot]], OFFSETS[slot])
            found.add((hop, 0))
            found.add((minus(ORIGIN, hop), 0))
    return sorted(found)


def kernel(
    ids_ref, emb_ref, out_ref,
    emb, ids, buf, idb, idcol, idrow, racc, cacc, mat, res, rin,
    load, data_s, data_r, swap_s, swap_r, id_s, id_r, ids_s, ids_r, ret_s, ret_r,
):
    loads = [pltpu.make_async_copy(emb_ref, emb, load.at[0]), pltpu.make_async_copy(ids_ref, ids, load.at[1])]
    for one in loads:
        one.start()
    group = lax.axis_index("group")
    blk = lax.axis_index("blk")
    core = lax.rem(blk, 2)
    place = (lax.rem(group, 4), (blk // 16) * 2 + group // 4, lax.rem(blk // 2, 8))

    def device(offset, flip):
        x, y, z = (lax.rem(p + o, m) if o else p for p, o, m in zip(place, offset, SIZES))
        there = 1 - core if flip else core
        return (lax.rem(y, 2) * 4 + x, (y // 2) * 16 + z * 2 + there)

    barrier = pltpu.get_barrier_semaphore()
    everyone = partners()
    for offset, flip in everyone:
        pl.semaphore_signal(barrier, inc=1, device_id=device(offset, flip), device_id_type=MESH)

    def rows_of(slot, part, count):
        return pl.ds(pl.multiple_of(slot * CHIP + core * ROWS + part * PART, BLOCK), count)

    own = rows_of(0, 0, ROWS)
    for one in loads:
        one.wait()
    as_float = emb[...].astype(jnp.float32)
    total = jnp.sum(as_float * as_float, axis=1, keepdims=True)
    buf[own, :] = (as_float * lax.rsqrt(total + 1e-06)).astype(jnp.bfloat16)
    for block in range(BLOCKS):
        idb[0, core, pl.ds(block, 1), :] = jnp.full((1, LANES), ids[block], jnp.int32)
    idb[0, core, pl.ds(BLOCKS, BLOCK - BLOCKS), :] = jnp.full((BLOCK - BLOCKS, LANES), -1, jnp.int32)
    pl.semaphore_wait(barrier, len(everyone))

    def data_copy(slot, part):
        parent = PARENTS[part][slot]
        return pltpu.make_async_remote_copy(
            src_ref=buf.at[rows_of(parent, part, PART), :], dst_ref=buf.at[rows_of(slot, part, PART), :],
            send_sem=data_s.at[slot, part], recv_sem=data_r.at[slot, part],
            device_id=device(minus(OFFSETS[parent], OFFSETS[slot]), 0), device_id_type=MESH)

    def id_copy(slot):
        parent = PARENTS[0][slot]
        return pltpu.make_async_remote_copy(
            src_ref=idb.at[parent, core], dst_ref=idb.at[slot, core], send_sem=id_s.at[slot], recv_sem=id_r.at[slot],
            device_id=device(minus(OFFSETS[parent], OFFSETS[slot]), 0), device_id_type=MESH)

    def swap_copy(slot):
        return pltpu.make_async_remote_copy(
            src_ref=buf.at[rows_of(slot, 0, ROWS), :], dst_ref=buf.at[rows_of(slot, 0, ROWS), :],
            send_sem=swap_s.at[slot], recv_sem=swap_r.at[slot], device_id=device(ORIGIN, 1), device_id_type=MESH)

    def swap_ids(slot):
        return pltpu.make_async_remote_copy(
            src_ref=idb.at[slot, core], dst_ref=idb.at[slot, core], send_sem=ids_s.at[slot], recv_sem=ids_r.at[slot],
            device_id=device(ORIGIN, 1), device_id_type=MESH)

    def return_copy(slot, flip):
        return pltpu.make_async_remote_copy(
            src_ref=res.at[pl.ds(slot, 1), :], dst_ref=rin.at[pl.ds(slot * 2 + core, 1), :],
            send_sem=ret_s.at[slot, flip], recv_sem=ret_r.at[slot, core],
            device_id=device(OFFSETS[slot], flip), device_id_type=MESH)

    used = sorted(slot for group in FOLDS for slot in group)
    fan = [(slot, flip) for slot in used for flip in (0, 1) if (slot, flip) != (0, 0)]

    def merge(first, seconds, count, itself):
        left = pl.ds(pl.multiple_of(first, BLOCK), count)
        others = [buf[pl.ds(pl.multiple_of(one * CHIP, CHIP), CHIP), :] for one in seconds]
        right = jnp.concatenate(others, axis=0) if len(others) > 1 else others[0]
        scores = lax.dot_general(buf[left, :], right, NT, preferred_element_type=jnp.float32)
        mine = idcol[left, :]
        best = racc[left, :]
        for index, one in enumerate(seconds):
            top = pl.ds(pl.multiple_of(one * 8, 8), 8)
            theirs = idrow[pl.ds(pl.multiple_of(one * 8, 8), 1), :]
            tops = []
            for tile in range(CHIP // LANES):
                at = index * CHIP + tile * LANES
                allowed = mine == theirs[:, tile * LANES:(tile + 1) * LANES]
                if itself:
                    here = lax.broadcasted_iota(jnp.int32, (count, LANES), 0) + first
                    there = lax.broadcasted_iota(jnp.int32, (count, LANES), 1) + at
                    allowed = allowed & (here != there)
                kept = jnp.where(allowed, scores[:, at:at + LANES], NEG)
                best = jnp.maximum(best, kept)
                if not itself:
                    tops.append(jnp.max(kept.reshape(count // 8, 8, LANES), axis=0))
            if not itself:
                cacc[top, :] = jnp.maximum(cacc[top, :], jnp.concatenate(tops, axis=1))
        racc[left, :] = best

    def spread(slot, half):
        tile = idb[slot, half]
        wide = jnp.broadcast_to(tile[:BLOCKS, None, :], (BLOCKS, BLOCK, LANES)).reshape(ROWS, LANES)
        idcol[pl.ds(pl.multiple_of(slot * CHIP + half * ROWS, BLOCK), ROWS), :] = wide

    owner = lax.broadcasted_iota(jnp.int32, (8, LANES), 1) // BLOCK
    sub = lax.broadcasted_iota(jnp.int32, (8, LANES), 0)

    def across(slot):
        both = jnp.concatenate([idb[slot, 0][:BLOCKS], idb[slot, 1][:BLOCKS]], axis=0)
        tiles = [
            jnp.max(jnp.where(owner == sub, both[8 * tile:8 * tile + 8], -1), axis=0, keepdims=True)
            for tile in range(CHIP // LANES)
        ]
        idrow[pl.ds(slot * 8, 8), :] = jnp.broadcast_to(jnp.concatenate(tiles, axis=1), (8, CHIP))

    lanes = lax.broadcasted_iota(jnp.int32, (CHIP, LANES), 1)

    def fold(slots):
        for slot in slots:
            wide = racc[pl.ds(slot * CHIP, CHIP), :]
            mat[...] = jnp.where(lanes == slot, jnp.max(wide, axis=1, keepdims=True), mat[...])
        turned = jnp.transpose(mat[...])
        for slot in slots:
            tops = jnp.max(cacc[pl.ds(slot * 8, 8), :], axis=0, keepdims=True)
            res[pl.ds(slot, 1), :] = jnp.maximum(turned[slot:slot + 1], tops)
        for slot in slots:
            for flip in (0, 1):
                if (slot, flip) != (0, 0):
                    return_copy(slot, flip).start()

    arrived, here, have = set(), set(), set()

    def arrive(slot, part):
        if slot and (slot, part) not in arrived:
            arrived.add((slot, part))
            data_copy(slot, part).wait_recv()
            if part == 0:
                id_copy(slot).wait_recv()

    def need_half(slot):
        if slot not in here:
            here.add(slot)
            for part in range(PARTS):
                arrive(slot, part)
            spread(slot, core)

    def need(slot):
        need_half(slot)
        if slot not in have:
            have.add(slot)
            swap_copy(slot).wait_recv()
            swap_ids(slot).wait_recv()
            spread(slot, 1 - core)
            across(slot)

    swapped, started = [], False
    for kind, one, part in PROGRAM:
        if kind == SEND:
            arrive(PARENTS[part][one], part)
            if part == 0:
                id_copy(one).start()
            data_copy(one, part).start()
        elif kind == SWAP:
            for index in range(PARTS):
                arrive(one, index)
            swapped.append(one)
            swap_ids(one).start()
            swap_copy(one).start()
        elif kind == FOLD:
            fold(FOLDS[one])
        else:
            if not started:
                started = True
                racc[...] = jnp.full(racc.shape, NEG, jnp.float32)
                cacc[...] = jnp.full(cacc.shape, NEG, jnp.float32)
                mat[...] = jnp.full(mat.shape, NEG, jnp.float32)
                need(0)
                merge(core * ROWS, [0], ROWS, True)
            if len(STEPS[one]) == 1:
                (first, seconds), = STEPS[one]
                need_half(first)
                for slot in seconds:
                    need(slot)
                merge(first * CHIP + core * ROWS, seconds, ROWS, False)
            else:
                (p0, q0), (p1, q1) = STEPS[one]
                for slot in (p0, p1, *q0, *q1):
                    need(slot)
                merge((p0 + core * (p1 - p0)) * CHIP, [a + core * (b - a) for a, b in zip(q0, q1)], CHIP, False)

    rin[pl.ds(core, 1), :] = res[pl.ds(0, 1), :]

    def wait_return(slot, sender):
        pltpu.make_async_remote_copy(
            src_ref=res.at[pl.ds(slot, 1), :], dst_ref=rin.at[pl.ds(slot * 2 + sender, 1), :],
            send_sem=ret_s.at[slot, 0], recv_sem=ret_r.at[slot, sender],
            device_id=device(ORIGIN, 1), device_id_type=MESH).wait_recv()

    wait_return(0, 1 - core)
    for slot in used:
        for sender in (0, 1):
            if slot:
                wait_return(slot, sender)
    joined = functools.reduce(jnp.maximum, [rin[pl.ds(2 * slot, 2), :] for slot in used])
    joined = jnp.max(joined, axis=0, keepdims=True)
    out_ref[...] = jnp.where(core == 0, joined[:, :ROWS], joined[:, ROWS:])

    for slot, flip in fan:
        return_copy(slot, flip).wait_send()
    for slot in swapped:
        swap_ids(slot).wait_send()
        swap_copy(slot).wait_send()
    for slot in range(1, SLOTS):
        id_copy(slot).wait_send()
        for part in range(PARTS):
            data_copy(slot, part).wait_send()


def per_device(embeddings, block_cluster):
    vmem = pl.BlockSpec(memory_space=pltpu.VMEM)
    dma = pltpu.SemaphoreType.DMA
    out = pl.pallas_call(
        kernel,
        out_shape=jax.ShapeDtypeStruct((1, ROWS), jnp.float32),
        in_specs=[pl.BlockSpec(memory_space=pltpu.HBM)] * 2,
        out_specs=vmem,
        scratch_shapes=[
            pltpu.VMEM((ROWS, WIDTH), jnp.bfloat16),
            pltpu.SMEM((BLOCKS,), jnp.int32),
            pltpu.VMEM((SLOTS * CHIP, WIDTH), jnp.bfloat16),
            pltpu.VMEM((SLOTS, 2, BLOCK, LANES), jnp.int32),
            pltpu.VMEM((SLOTS * CHIP, LANES), jnp.int32),
            pltpu.VMEM((SLOTS * 8, CHIP), jnp.int32),
            pltpu.VMEM((SLOTS * CHIP, LANES), jnp.float32),
            pltpu.VMEM((SLOTS * 8, CHIP), jnp.float32),
            pltpu.VMEM((CHIP, LANES), jnp.float32),
            pltpu.VMEM((SLOTS, CHIP), jnp.float32),
            pltpu.VMEM((SLOTS * 2, CHIP), jnp.float32),
            dma((2,)),
            dma((SLOTS, PARTS)), dma((SLOTS, PARTS)),
            dma((SLOTS,)), dma((SLOTS,)),
            dma((SLOTS,)), dma((SLOTS,)),
            dma((SLOTS,)), dma((SLOTS,)),
            dma((SLOTS, 2)), dma((SLOTS, 2)),
        ],
        compiler_params=pltpu.CompilerParams(
            collective_id=0, has_side_effects=True, vmem_limit_bytes=40 * 2**20),
    )(block_cluster, embeddings)
    return out.reshape(ROWS)


def solution(mesh):
    return jax.shard_map(
        per_device, mesh=mesh, in_specs=(P(("group", "blk"), None), P(("group", "blk"))), out_specs=P(("group", "blk")),
        check_vma=False,
    )
```

```python
import functools

import jax
import jax.numpy as jnp
from jax import lax
from jax.experimental import pallas as pl
from jax.experimental.pallas import tpu as pltpu
from jax.sharding import PartitionSpec as P

MESH = pl.DeviceIdType.MESH
SIZES = (4, 4, 8)
ROWS = 192
CHIP = 2 * ROWS
BLOCK = 16
BLOCKS = ROWS // BLOCK
WIDTH = 1024
LANES = 128
NEG = float("-inf")
NT = (((1,), (1,)), ((), ()))

SEND, SWAP, STEP, FOLD = range(4)
OFFSETS = (
    (0, 0, 0), (3, 0, 0), (1, 1, 0), (2, 1, 0), (3, 3, 0), (0, 0, 1), (0, 1, 1), (0, 2, 1),
    (0, 3, 1), (0, 0, 2), (0, 2, 2), (0, 3, 2), (0, 0, 6), (1, 0, 6), (2, 0, 6), (3, 0, 6),
)
PARENTS = (
    (-1, 0, 0, 2, 1, 0, 5, 6, 11, 5, 11, 9, 0, 14, 15, 12),
    (-1, 0, 0, 2, 1, 0, 5, 6, 11, 5, 11, 9, 15, 12, 15, 1),
    (-1, 0, 0, 2, 0, 0, 5, 8, 0, 5, 7, 8, 0, 12, 13, 12),
)
PROGRAM = (
    (SEND, 1, 0), (SEND, 2, 0), (SEND, 5, 0), (SEND, 8, 2), (SEND, 12, 0), (SWAP, 0, 0), (SEND, 4, 2),
    (SEND, 2, 2), (SEND, 1, 1), (SEND, 2, 1), (SEND, 5, 1), (SEND, 12, 2), (SEND, 4, 0), (SEND, 1, 2),
    (SEND, 3, 0), (SEND, 6, 0), (SEND, 9, 0), (SEND, 7, 2), (SEND, 15, 0), (SEND, 3, 2), (SEND, 4, 1),
    (SEND, 6, 1), (SEND, 9, 1), (SEND, 15, 1), (SWAP, 2, 0), (SEND, 3, 1), (SEND, 5, 2), (SWAP, 1, 0),
    (SEND, 11, 0), (SEND, 7, 0), (SEND, 15, 2), (SEND, 11, 2), (SEND, 13, 2), (SWAP, 4, 0), (SEND, 11, 1),
    (SEND, 14, 0), (SEND, 7, 1), (STEP, 0, 0), (SWAP, 3, 0), (SWAP, 5, 0), (SEND, 9, 2), (SEND, 6, 2),
    (SEND, 8, 0), (SEND, 10, 0), (SEND, 12, 1), (SWAP, 15, 0), (SEND, 14, 1), (SEND, 10, 2), (STEP, 1, 0),
    (SEND, 14, 2), (SWAP, 11, 0), (SEND, 8, 1), (SEND, 10, 1), (SWAP, 7, 0), (SEND, 13, 0), (STEP, 2, 0),
    (STEP, 3, 0), (STEP, 4, 0), (SWAP, 9, 0), (SWAP, 12, 0), (SEND, 13, 1), (SWAP, 6, 0), (STEP, 5, 0),
    (STEP, 6, 0), (STEP, 7, 0), (SWAP, 8, 0), (SWAP, 14, 0), (SWAP, 10, 0), (STEP, 8, 0), (STEP, 9, 0),
    (STEP, 10, 0), (SWAP, 13, 0), (STEP, 11, 0), (STEP, 12, 0), (STEP, 13, 0), (STEP, 14, 0), (STEP, 15, 0),
    (FOLD, 0, 0), (STEP, 16, 0), (FOLD, 1, 0), (STEP, 17, 0), (FOLD, 2, 0),
)
STEPS = (
    ((2, (0, 1)), (4, (1, 2))),
    ((3, (1, 4)), (5, (3, 4))),
    ((15, (1, 4)), (15, (0, 3))),
    ((15, (2, 5)), (5, (2, 0))),
    ((11, (5, 1)), (11, (2, 3))),
    ((11, (15, 7)), (7, (0, 1))),
    ((7, (4, 2)), (7, (3, 5))),
    ((15, (7, 9)), (9, (3, 2))),
    ((12, (7, 11)), (6, (3, 15))),
    ((9, (4, 12)), (12, (1, 5))),
    ((8, (3, 15)), (6, (2, 12))),
    ((14, (0, 3)), (14, (5, 6))),
    ((14, (7, 8)), (14, (9, 11))),
    ((12, (14, 10)), (10, (0, 1))),
    ((10, (15, 14)), (13, (5, 6))),
    ((13, (7, 8)), (8, (2, 12))),
    ((13, (11,)), (1, (0,))),
    ((5, (1,)),),
)
FOLDS = ((10, 14, 3, 7, 15, 2, 4, 6, 8, 9, 12), (11, 13, 0), (1, 5))

SLOTS = len(OFFSETS)
PARTS = len(PARENTS)
PART = ROWS // PARTS


def minus(a, b):
    return tuple((p - q) % m for p, q, m in zip(a, b, SIZES))


ORIGIN = (0, 0, 0)


def partners():
    found = {(ORIGIN, 1)}
    for parents in PARENTS:
        for slot in range(1, SLOTS):
            hop = minus(OFFSETS[parents[slot]], OFFSETS[slot])
            found.add((hop, 0))
            found.add((minus(ORIGIN, hop), 0))
    return sorted(found)


def kernel(
    ids_ref, emb_ref, out_ref,
    emb, ids, buf, idb, idcol, idrow, racc, cacc, mat, res, rin,
    load, data_s, data_r, swap_s, swap_r, id_s, id_r, ids_s, ids_r, ret_s, ret_r,
):
    loads = [pltpu.make_async_copy(emb_ref, emb, load.at[0]), pltpu.make_async_copy(ids_ref, ids, load.at[1])]
    for one in loads:
        one.start()
    group = lax.axis_index("group")
    blk = lax.axis_index("blk")
    core = lax.rem(blk, 2)
    place = (lax.rem(group, 4), (blk // 16) * 2 + group // 4, lax.rem(blk // 2, 8))

    def device(offset, flip):
        x, y, z = (lax.rem(p + o, m) if o else p for p, o, m in zip(place, offset, SIZES))
        there = 1 - core if flip else core
        return (lax.rem(y, 2) * 4 + x, (y // 2) * 16 + z * 2 + there)

    barrier = pltpu.get_barrier_semaphore()
    everyone = partners()
    for offset, flip in everyone:
        pl.semaphore_signal(barrier, inc=1, device_id=device(offset, flip), device_id_type=MESH)

    def rows_of(slot, part, count):
        return pl.ds(pl.multiple_of(slot * CHIP + core * ROWS + part * PART, BLOCK), count)

    own = rows_of(0, 0, ROWS)
    for one in loads:
        one.wait()
    as_float = emb[...].astype(jnp.float32)
    total = jnp.sum(as_float * as_float, axis=1, keepdims=True)
    buf[own, :] = (as_float * lax.rsqrt(total + 1e-06)).astype(jnp.bfloat16)
    for block in range(BLOCKS):
        idb[0, core, pl.ds(block, 1), :] = jnp.full((1, LANES), ids[block], jnp.int32)
    idb[0, core, pl.ds(BLOCKS, BLOCK - BLOCKS), :] = jnp.full((BLOCK - BLOCKS, LANES), -1, jnp.int32)
    pl.semaphore_wait(barrier, len(everyone))

    def data_copy(slot, part):
        parent = PARENTS[part][slot]
        return pltpu.make_async_remote_copy(
            src_ref=buf.at[rows_of(parent, part, PART), :], dst_ref=buf.at[rows_of(slot, part, PART), :],
            send_sem=data_s.at[slot, part], recv_sem=data_r.at[slot, part],
            device_id=device(minus(OFFSETS[parent], OFFSETS[slot]), 0), device_id_type=MESH)

    def id_copy(slot):
        parent = PARENTS[0][slot]
        return pltpu.make_async_remote_copy(
            src_ref=idb.at[parent], dst_ref=idb.at[slot], send_sem=id_s.at[slot], recv_sem=id_r.at[slot],
            device_id=device(minus(OFFSETS[parent], OFFSETS[slot]), 0), device_id_type=MESH)

    def swap_copy(slot):
        return pltpu.make_async_remote_copy(
            src_ref=buf.at[rows_of(slot, 0, ROWS), :], dst_ref=buf.at[rows_of(slot, 0, ROWS), :],
            send_sem=swap_s.at[slot], recv_sem=swap_r.at[slot], device_id=device(ORIGIN, 1), device_id_type=MESH)

    def swap_ids(slot):
        return pltpu.make_async_remote_copy(
            src_ref=idb.at[slot, core], dst_ref=idb.at[slot, core], send_sem=ids_s.at[slot], recv_sem=ids_r.at[slot],
            device_id=device(ORIGIN, 1), device_id_type=MESH)

    def return_copy(slot, flip):
        return pltpu.make_async_remote_copy(
            src_ref=res.at[pl.ds(slot, 1), :], dst_ref=rin.at[pl.ds(slot * 2 + core, 1), :],
            send_sem=ret_s.at[slot, flip], recv_sem=ret_r.at[slot, core],
            device_id=device(OFFSETS[slot], flip), device_id_type=MESH)

    used = sorted(slot for group in FOLDS for slot in group)
    fan = [(slot, flip) for slot in used for flip in (0, 1) if (slot, flip) != (0, 0)]

    def merge(first, seconds, count, itself):
        left = pl.ds(pl.multiple_of(first, BLOCK), count)
        others = [buf[pl.ds(pl.multiple_of(one * CHIP, CHIP), CHIP), :] for one in seconds]
        right = jnp.concatenate(others, axis=0) if len(others) > 1 else others[0]
        scores = lax.dot_general(buf[left, :], right, NT, preferred_element_type=jnp.float32)
        mine = idcol[left, :]
        best = racc[left, :]
        for index, one in enumerate(seconds):
            top = pl.ds(pl.multiple_of(one * 8, 8), 8)
            theirs = idrow[pl.ds(pl.multiple_of(one * 8, 8), 1), :]
            tops = []
            for tile in range(CHIP // LANES):
                at = index * CHIP + tile * LANES
                allowed = mine == theirs[:, tile * LANES:(tile + 1) * LANES]
                if itself:
                    here = lax.broadcasted_iota(jnp.int32, (count, LANES), 0) + first
                    there = lax.broadcasted_iota(jnp.int32, (count, LANES), 1) + at
                    allowed = allowed & (here != there)
                kept = jnp.where(allowed, scores[:, at:at + LANES], NEG)
                best = jnp.maximum(best, kept)
                if not itself:
                    tops.append(jnp.max(kept.reshape(count // 8, 8, LANES), axis=0))
            if not itself:
                cacc[top, :] = jnp.maximum(cacc[top, :], jnp.concatenate(tops, axis=1))
        racc[left, :] = best

    def spread(slot, half):
        tile = idb[slot, half]
        wide = jnp.broadcast_to(tile[:BLOCKS, None, :], (BLOCKS, BLOCK, LANES)).reshape(ROWS, LANES)
        idcol[pl.ds(pl.multiple_of(slot * CHIP + half * ROWS, BLOCK), ROWS), :] = wide

    owner = lax.broadcasted_iota(jnp.int32, (8, LANES), 1) // BLOCK
    sub = lax.broadcasted_iota(jnp.int32, (8, LANES), 0)

    def across(slot):
        both = jnp.concatenate([idb[slot, 0][:BLOCKS], idb[slot, 1][:BLOCKS]], axis=0)
        tiles = [
            jnp.max(jnp.where(owner == sub, both[8 * tile:8 * tile + 8], -1), axis=0, keepdims=True)
            for tile in range(CHIP // LANES)
        ]
        idrow[pl.ds(slot * 8, 8), :] = jnp.broadcast_to(jnp.concatenate(tiles, axis=1), (8, CHIP))

    lanes = lax.broadcasted_iota(jnp.int32, (CHIP, LANES), 1)

    def fold(slots):
        for slot in slots:
            wide = racc[pl.ds(slot * CHIP, CHIP), :]
            mat[...] = jnp.where(lanes == slot, jnp.max(wide, axis=1, keepdims=True), mat[...])
        turned = jnp.transpose(mat[...])
        for slot in slots:
            tops = jnp.max(cacc[pl.ds(slot * 8, 8), :], axis=0, keepdims=True)
            res[pl.ds(slot, 1), :] = jnp.maximum(turned[slot:slot + 1], tops)
        for slot in slots:
            for flip in (0, 1):
                if (slot, flip) != (0, 0):
                    return_copy(slot, flip).start()

    arrived, here, have = set(), set(), set()

    def arrive(slot, part):
        if slot and (slot, part) not in arrived:
            arrived.add((slot, part))
            data_copy(slot, part).wait_recv()
            if part == 0:
                id_copy(slot).wait_recv()

    def need_half(slot):
        if slot not in here:
            here.add(slot)
            for part in range(PARTS):
                arrive(slot, part)
            spread(slot, core)

    def need(slot):
        need_half(slot)
        if slot not in have:
            have.add(slot)
            swap_copy(slot).wait_recv()
            spread(slot, 1 - core)
            across(slot)

    swapped, started, paired, waiting = [], False, False, []
    swap_ids(0).start()
    for kind, one, part in PROGRAM:
        if not paired and (kind != SEND or PARENTS[part][one]):
            paired = True
            swap_ids(0).wait_recv()
            for slot in waiting:
                id_copy(slot).start()
        if kind == SEND:
            arrive(PARENTS[part][one], part)
            if part == 0 and paired:
                id_copy(one).start()
            elif part == 0:
                waiting.append(one)
            data_copy(one, part).start()
        elif kind == SWAP:
            for index in range(PARTS):
                arrive(one, index)
            swapped.append(one)
            swap_copy(one).start()
        elif kind == FOLD:
            fold(FOLDS[one])
        else:
            if not started:
                started = True
                racc[...] = jnp.full(racc.shape, NEG, jnp.float32)
                cacc[...] = jnp.full(cacc.shape, NEG, jnp.float32)
                mat[...] = jnp.full(mat.shape, NEG, jnp.float32)
                need(0)
                merge(core * ROWS, [0], ROWS, True)
            if len(STEPS[one]) == 1:
                (first, seconds), = STEPS[one]
                need_half(first)
                for slot in seconds:
                    need(slot)
                merge(first * CHIP + core * ROWS, seconds, ROWS, False)
            else:
                (p0, q0), (p1, q1) = STEPS[one]
                for slot in (p0, p1, *q0, *q1):
                    need(slot)
                merge((p0 + core * (p1 - p0)) * CHIP, [a + core * (b - a) for a, b in zip(q0, q1)], CHIP, False)

    rin[pl.ds(core, 1), :] = res[pl.ds(0, 1), :]

    def wait_return(slot, sender):
        pltpu.make_async_remote_copy(
            src_ref=res.at[pl.ds(slot, 1), :], dst_ref=rin.at[pl.ds(slot * 2 + sender, 1), :],
            send_sem=ret_s.at[slot, 0], recv_sem=ret_r.at[slot, sender],
            device_id=device(ORIGIN, 1), device_id_type=MESH).wait_recv()

    wait_return(0, 1 - core)
    for slot in used:
        for sender in (0, 1):
            if slot:
                wait_return(slot, sender)
    joined = functools.reduce(jnp.maximum, [rin[pl.ds(2 * slot, 2), :] for slot in used])
    joined = jnp.max(joined, axis=0, keepdims=True)
    out_ref[...] = jnp.where(core == 0, joined[:, :ROWS], joined[:, ROWS:])

    for slot, flip in fan:
        return_copy(slot, flip).wait_send()
    swap_ids(0).wait_send()
    for slot in swapped:
        swap_copy(slot).wait_send()
    for slot in range(1, SLOTS):
        id_copy(slot).wait_send()
        for part in range(PARTS):
            data_copy(slot, part).wait_send()


def per_device(embeddings, block_cluster):
    vmem = pl.BlockSpec(memory_space=pltpu.VMEM)
    dma = pltpu.SemaphoreType.DMA
    out = pl.pallas_call(
        kernel,
        out_shape=jax.ShapeDtypeStruct((1, ROWS), jnp.float32),
        in_specs=[pl.BlockSpec(memory_space=pltpu.HBM)] * 2,
        out_specs=vmem,
        scratch_shapes=[
            pltpu.VMEM((ROWS, WIDTH), jnp.bfloat16),
            pltpu.SMEM((BLOCKS,), jnp.int32),
            pltpu.VMEM((SLOTS * CHIP, WIDTH), jnp.bfloat16),
            pltpu.VMEM((SLOTS, 2, BLOCK, LANES), jnp.int32),
            pltpu.VMEM((SLOTS * CHIP, LANES), jnp.int32),
            pltpu.VMEM((SLOTS * 8, CHIP), jnp.int32),
            pltpu.VMEM((SLOTS * CHIP, LANES), jnp.float32),
            pltpu.VMEM((SLOTS * 8, CHIP), jnp.float32),
            pltpu.VMEM((CHIP, LANES), jnp.float32),
            pltpu.VMEM((SLOTS, CHIP), jnp.float32),
            pltpu.VMEM((SLOTS * 2, CHIP), jnp.float32),
            dma((2,)),
            dma((SLOTS, PARTS)), dma((SLOTS, PARTS)),
            dma((SLOTS,)), dma((SLOTS,)),
            dma((SLOTS,)), dma((SLOTS,)),
            dma((SLOTS,)), dma((SLOTS,)),
            dma((SLOTS, 2)), dma((SLOTS, 2)),
        ],
        compiler_params=pltpu.CompilerParams(
            collective_id=0, has_side_effects=True, vmem_limit_bytes=40 * 2**20),
    )(block_cluster, embeddings)
    return out.reshape(ROWS)


def solution(mesh):
    return jax.shard_map(
        per_device, mesh=mesh, in_specs=(P(("group", "blk"), None), P(("group", "blk"))), out_specs=P(("group", "blk")),
        check_vma=False,
    )
```
